32 devices in a mesh: wide: 8 (over y, x, core), grp: 4 (over z).
Axes of the slice: x: 2, y: 2, z: 4, core: 2. Of those that a mesh axis runs over, the one named last changes fastest.
Arguments:
- solution: float32 [64, 32768], P(None, ('wide', 'grp')), may hold values from -6 to 6
- incident: float32 [64, 32768], P(None, ('wide', 'grp')), may hold values from -12 to 12
- leaf_blocks: float32 [512, 32768], P(None, ('wide', 'grp')), may hold values from -0.25 to 0.25
- leaf_inverse: float32 [512, 32768], P(None, ('wide', 'grp')), may hold values from -0.25 to 0.25
- col_basis: float32 [6, 96, 32768], P(None, None, ('wide', 'grp')), may hold values from -0.625 to 0.625
- row_basis: float32 [6, 96, 32768], P(None, None, ('wide', 'grp')), may hold values from -6 to 6
Outputs:
- refined: float32 [64, 32768], P(None, ('wide', 'grp'))
- residual: float32 [64, 32768], P(None, ('wide', 'grp'))
The draws below stay inside these ranges and needn't reach their ends.
All inputs are finite; a program needn't handle non-finite values.
Results may differ from the reference program's by a relative error of at most 0.0001.
Values sent between devices are 32-bit elements; how exact they have to be, the bound alone decides.
No kernel may reach another device: no remote copies, remote signals or barrier semaphores. Data moves between devices by JAX's collectives and lax.ppermute only.
A program may use at most 64 MiB of HBM per device.

```python
import jax
import jax.numpy as jnp
from jax import lax

LEAF = 512
RANK = 96
COLS = 64
LEVELS = 6
ORDER = 32768


def draw_row_basis(key, part):
    levels = jnp.arange(LEVELS).astype(jnp.float32)
    scales = (LEAF * 2.0 ** levels) ** (-0.5)
    base = jnp.clip(jax.random.normal(key, (LEVELS, RANK, ORDER), jnp.float32), -6.0, 6.0)
    return base * scales[:, None, None]


def level_of(key, extent, cuts, low, largest):
    level = 1.0
    for dim, shards_of in cuts:
        draws = jax.random.uniform(jax.random.fold_in(jax.random.fold_in(key, 6), dim), (shards_of,), jnp.float32, low / len(cuts), largest / len(cuts))
        level = level * jnp.repeat(jnp.exp(draws), extent[dim] // shards_of).reshape((-1,) + (1,) * (len(extent) - 1 - dim))
    return level


def bell_draw(stream_key, extent, spread, limit, shards=(), kind=jnp.bfloat16):
    values = jax.random.normal(stream_key, extent, jnp.float32) * spread
    if len(shards) > 0:
        values = level_of(stream_key, extent, shards, -0.22, 0.18) * values
    return jnp.clip(values, min=-limit, max=limit).astype(kind)


def setup_inputs(seed: int = 0) -> dict:
    key_list = jax.random.split(jax.random.key(seed), 7)
    return {
        "solution": bell_draw(key_list[0], (COLS, ORDER), 1.0, 6.0, ((1, 32),), jnp.float32),
        "incident": bell_draw(key_list[1], (COLS, ORDER), 2.0, 12.0, ((1, 32),), jnp.float32),
        "leaf_blocks": bell_draw(key_list[2], (LEAF, ORDER), LEAF ** -0.5, 0.25, ((1, 32),), jnp.float32),
        "leaf_inverse": bell_draw(key_list[3], (LEAF, ORDER), LEAF ** -0.5, 0.25, ((1, 32),), jnp.float32),
        "col_basis": bell_draw(key_list[4], (LEVELS, RANK, ORDER), RANK ** -0.5, 0.625, ((2, 32),), jnp.float32),
        "row_basis": draw_row_basis(jax.random.fold_in(key_list[6], 71), 0),
    }


def leaf_apply(field, blocks):
    cols, order = field.shape
    leaf = blocks.shape[0]
    count = order // leaf
    pieces = field.reshape(cols, count, leaf)
    tables = blocks.reshape(leaf, count, leaf)
    image = jnp.einsum("pkj,jki->pki", pieces, tables, precision=lax.Precision.HIGHEST)
    return image.reshape(cols, order)


def operator(field, leaf_blocks, col_basis, row_basis):
    cols, order = field.shape
    leaf = leaf_blocks.shape[0]
    image = leaf_apply(field, leaf_blocks)
    for level in range(LEVELS):
        node = leaf * 2 ** level
        count = order // node
        pieces = field.reshape(cols, count, node)
        rights = row_basis[level].reshape(RANK, count, node)
        coefs = jnp.einsum("pks,rks->kpr", pieces, rights, precision=lax.Precision.HIGHEST)
        coefs = coefs.reshape(count // 2, 2, cols, RANK)[:, ::-1].reshape(count, cols, RANK)
        lefts = col_basis[level].reshape(RANK, count, node)
        image = image + jnp.einsum("kpr,rks->pks", coefs, lefts, precision=lax.Precision.HIGHEST).reshape(cols, order)
    return image


def reference(solution, incident, leaf_blocks, leaf_inverse, col_basis, row_basis):
    first_residual = incident - operator(solution, leaf_blocks, col_basis, row_basis)
    refined = solution + leaf_apply(first_residual, leaf_inverse)
    residual = incident - operator(refined, leaf_blocks, col_basis, row_basis)
    return refined, residual
```

```python
import jax
import jax.numpy as jnp
from jax import lax
from jax.sharding import PartitionSpec as P

AXES = ("wide", "grp")
DOT = lax.Precision.HIGH


def bits_of(axis):
    return lax.axis_size(axis).bit_length() - 1


def parity(number):
    return number.bit_count() & 1


def swap(block, masks):
    wides, grps = lax.axis_size("wide"), lax.axis_size("grp")
    route = []
    for w in range(wides):
        for g in range(grps):
            wide_mask, grp_mask = masks[parity(w) ^ parity(g)]
            route.append((w * grps + g, (w ^ wide_mask) * grps + (g ^ grp_mask)))
    return lax.ppermute(block, AXES, route)


def both(wide_mask, grp_mask):
    return ((wide_mask, grp_mask), (wide_mask, grp_mask))


def climb_tree(partials):
    gathered = []
    pending = partials
    masks = [both(0, 1 << b) for b in range(bits_of("grp"))]
    masks += [both(1 << b, 0) for b in range(bits_of("wide"))]
    for mask in masks:
        received = swap(pending, mask)
        gathered.append(received[0])
        pending = (pending + received)[1:]
    return jnp.stack(gathered)


def in_lanes(partials):
    low = partials[:3]
    wide, grp = lax.axis_index("wide"), lax.axis_index("grp")
    ones = wide ^ (wide >> 1) ^ (wide >> 2) ^ grp ^ (grp >> 1)
    first = (ones & 1) == 0
    fourth, fifth = partials[3], partials[4]
    mine = jnp.where(first, fourth, fifth) + swap(jnp.where(first, fifth, fourth), both(1, 0))
    low_got = swap(low, both(0, 1))
    low_next = (low + low_got)[1:]
    mine = mine + swap(mine, both(1, 1))
    mine = mine + swap(mine, both(1, 2))
    low_got_next = swap(low_next, both(0, 2))
    third = (low_next + low_got_next)[1]
    across = swap(mine, ((3, 0), (5, 0)))
    corner = swap(mine, both(6, 0))
    third = swap(third, both(1, 0))
    result = jnp.where(first, across, across + corner)
    other = swap(result, both(1, 0))
    return jnp.stack(
        [low_got[0], low_got_next[0], third, jnp.where(first, result, other), jnp.where(first, other, result)]
    )


def exchange(partials):
    if bits_of("grp") == 2 and bits_of("wide") == 3:
        return in_lanes(partials)
    return climb_tree(partials)


def leaf_apply(field, blocks):
    cols, rows = field.shape
    leaf = blocks.shape[0]
    count = rows // leaf
    pieces = field.reshape(cols, count, leaf)
    tables = blocks.reshape(leaf, count, leaf)
    image = jnp.einsum("pkj,jki->pki", pieces, tables, precision=DOT)
    return image.reshape(cols, rows)


def near_field(field, leaf_blocks, col_basis, row_basis):
    cols, rows = field.shape
    leaf = leaf_blocks.shape[0]
    image = leaf_apply(field, leaf_blocks)
    pieces = field.reshape(cols, 2, leaf)
    rights = row_basis[0].reshape(row_basis.shape[1], 2, leaf)
    lefts = col_basis[0].reshape(col_basis.shape[1], 2, leaf)
    leaf_coefs = jnp.einsum("pks,rks->kpr", pieces, rights, precision=DOT)[::-1]
    return image + jnp.einsum("kpr,rks->pks", leaf_coefs, lefts, precision=DOT).reshape(cols, rows)


def residual_of(field, incident, leaf_blocks, col_basis, row_basis):
    partials = jnp.einsum("pn,lrn->lpr", field, row_basis[1:], precision=DOT)
    coefs = exchange(partials)
    near = incident - near_field(field, leaf_blocks, col_basis, row_basis)
    return near - jnp.einsum("lpr,lrn->pn", coefs, col_basis[1:], precision=DOT)


def per_device(solution, incident, leaf_blocks, leaf_inverse, col_basis, row_basis):
    first_residual = residual_of(solution, incident, leaf_blocks, col_basis, row_basis)
    refined = solution + leaf_apply(first_residual, leaf_inverse)
    residual = residual_of(refined, incident, leaf_blocks, col_basis, row_basis)
    return (refined, residual)


def solution(mesh):
    in_specs = (
        P(None, ("wide", "grp")),
        P(None, ("wide", "grp")),
        P(None, ("wide", "grp")),
        P(None, ("wide", "grp")),
        P(None, None, ("wide", "grp")),
        P(None, None, ("wide", "grp")),
    )
    out_specs = (P(None, ("wide", "grp")), P(None, ("wide", "grp")))
    return jax.shard_map(
        per_device, mesh=mesh, in_specs=in_specs, out_specs=out_specs, check_vma=False
    )
```

```python
import functools

import jax
import jax.numpy as jnp
from jax import lax
from jax.experimental import pallas as pl
from jax.experimental.pallas import tpu as pltpu
from jax.sharding import PartitionSpec as P

AXES = ("wide", "grp")
LANES = 128
TOP = 2
VMEM = pltpu.VMEM
F32 = jnp.float32
ROWS_OF_BOTH = (((1,), (1,)), ((), ()))
PLAIN = (((1,), (0,)), ((), ()))


def bits_of(axis):
    return lax.axis_size(axis).bit_length() - 1


def parity(number):
    return number.bit_count() & 1


def swap(block, masks):
    wides, grps = lax.axis_size("wide"), lax.axis_size("grp")
    route = []
    for w in range(wides):
        for g in range(grps):
            wide_mask, grp_mask = masks[parity(w) ^ parity(g)]
            route.append((w * grps + g, (w ^ wide_mask) * grps + (g ^ grp_mask)))
    return lax.ppermute(block, AXES, route)


def both(wide_mask, grp_mask):
    return ((wide_mask, grp_mask), (wide_mask, grp_mask))


def climb_tree(low, top, near_of, apply):
    gathered = []
    pending = jnp.concatenate([low, top])
    masks = [both(0, 1 << b) for b in range(bits_of("grp"))]
    masks += [both(1 << b, 0) for b in range(bits_of("wide"))]
    for mask in masks:
        received = swap(pending, mask)
        gathered.append(received[0])
        pending = (pending + received)[1:]
    near, *others = near_of()
    near = apply(1, near, jnp.stack(gathered[:-TOP]))
    return near, 1 + len(gathered) - TOP, jnp.stack(gathered[-TOP:]), others


def in_lanes(low, top, near_of, apply):
    wide, grp = lax.axis_index("wide"), lax.axis_index("grp")
    ones = wide ^ (wide >> 1) ^ (wide >> 2) ^ grp ^ (grp >> 1)
    first = (ones & 1) == 0
    fourth, fifth = top[0], top[1]
    mine = jnp.where(first, fourth, fifth) + swap(jnp.where(first, fifth, fourth), both(1, 0))
    low_got = swap(low, both(0, 1))
    low_next = (low + low_got)[1:]
    mine = mine + swap(mine, both(1, 1))
    near, *others = near_of()
    mine = mine + swap(mine, both(1, 2))
    low_got_next = swap(low_next, both(0, 2))
    third = (low_next + low_got_next)[1]
    across = swap(mine, ((3, 0), (5, 0)))
    corner = swap(mine, both(6, 0))
    across, third = lax.optimization_barrier((across, third))
    near = apply(1, near, jnp.stack([low_got[0], low_got_next[0]]))
    result = jnp.where(first, across, across + corner)
    other, third = swap(jnp.stack([result, third]), both(1, 0))
    return near, 3, jnp.stack([third, jnp.where(first, result, other), jnp.where(first, other, result)]), others


def exchange(low, top, near_of, apply):
    if bits_of("grp") == 2 and bits_of("wide") == 3:
        return in_lanes(low, top, near_of, apply)
    return climb_tree(low, top, near_of, apply)


def split(x):
    high = x.astype(jnp.bfloat16)
    return high, (x - high.astype(F32)).astype(jnp.bfloat16)


def dot(x, table, dims):
    count = x.shape[0]
    x_high, x_low = split(x)
    t_high, t_low = split(table)
    main = lax.dot_general(jnp.concatenate([x_high, x_low]), t_high, dims, preferred_element_type=F32)
    rest = lax.dot_general(x_high, t_low, dims, preferred_element_type=F32)
    return main[:count] + (main[count:] + rest)


def merged(basis):
    return basis.reshape(-1, basis.shape[-1])


def chunks_of(rank):
    widths = [LANES] * (rank // LANES)
    return widths + [w for w in (1 << b for b in reversed(range(LANES.bit_length() - 1))) if rank % LANES & w]


def packed_rows(cols, rank):
    return cols * rank // LANES


def pack(block):
    cols, rank = block.shape
    out, at = [], 0
    for w in chunks_of(rank):
        rows = cols * w // LANES
        piece = block[:, at : at + w]
        out.append(jnp.concatenate([piece[r : r + rows] for r in range(0, cols, rows)], axis=1))
        at += w
    return jnp.concatenate(out)


def unpack(dense, cols):
    out, at = [], 0
    for w in chunks_of(dense.shape[0] * LANES // cols):
        rows = cols * w // LANES
        piece = dense[at : at + rows]
        out.append(jnp.concatenate([piece[:, l : l + w] for l in range(0, LANES, w)]))
        at += rows
    return jnp.concatenate(out, axis=1)


def side_by_side(coefs, cols):
    return jnp.concatenate([unpack(coefs[l], cols) for l in range(coefs.shape[0])], axis=1)


def store_levels(ref, wide_block):
    rank = wide_block.shape[1] // ref.shape[0]
    for l in range(ref.shape[0]):
        ref[l] = pack(wide_block[:, l * rank : (l + 1) * rank])


def leaf_slices(blocks):
    leaf, rows = blocks.shape
    return [slice(s, s + leaf) for s in range(0, rows, leaf)]


def near_kernel(field, incident, leaf_blocks, col_basis, row_basis, near):
    pieces = leaf_slices(leaf_blocks)
    coefs = [dot(field[:, s], row_basis[0, :, s], ROWS_OF_BOTH) for s in pieces]
    for k, s in enumerate(pieces):
        image = dot(field[:, s], leaf_blocks[:, s], PLAIN)
        near[:, s] = incident[:, s] - image - dot(coefs[k ^ 1], col_basis[0, :, s], PLAIN)


def near_and_copy_kernel(field, incident, leaf_blocks, col_basis, row_basis, near, copy):
    copy[...] = field[...]
    near_kernel(field, incident, leaf_blocks, col_basis, row_basis, near)


def first_top_kernel(field_hbm, row_hbm, top, field, row, sems):
    levels = row_hbm.shape[0]
    copies = [pltpu.make_async_copy(field_hbm, field, sems.at[levels])]
    copies += [pltpu.make_async_copy(row_hbm.at[l], row.at[l], sems.at[l]) for l in reversed(range(levels))]
    for c in copies:
        c.start()
    for c in copies[: TOP + 1]:
        c.wait()
    store_levels(top, dot(field[...], merged(row[levels - TOP :]), ROWS_OF_BOTH))
    for c in copies[TOP + 1 :]:
        c.wait()


def low_kernel(field, row_basis, low):
    store_levels(low, dot(field[...], merged(row_basis[1 : row_basis.shape[0] - TOP]), ROWS_OF_BOTH))


def apply_kernel(start, near, coefs, col_basis, out):
    table = merged(col_basis[start : start + coefs.shape[0]])
    out[...] = near[...] - dot(side_by_side(coefs, near.shape[0]), table, PLAIN)


def refine_kernel(start, near, coefs, field, col_basis, leaf_inverse, row_basis, refined, top):
    levels = col_basis.shape[0]
    table = merged(col_basis[start:])
    first = near[...] - dot(side_by_side(coefs, near.shape[0]), table, PLAIN)
    for s in leaf_slices(leaf_inverse):
        refined[:, s] = field[:, s] + dot(first[:, s], leaf_inverse[:, s], PLAIN)
    store_levels(top, dot(refined[...], merged(row_basis[levels - TOP :]), ROWS_OF_BOTH))


def last_kernel(start, near, coefs, col_basis, out_hbm, out, sems):
    coefs = side_by_side(coefs, near.shape[0])
    rows = near.shape[1]
    step = rows // sems.shape[0]
    copies = []
    for k in range(sems.shape[0]):
        s = slice(k * step, k * step + step)
        out[:, s] = near[:, s] - dot(coefs, merged(col_basis[start:, :, s]), PLAIN)
        copies.append(pltpu.make_async_copy(out.at[:, s], out_hbm.at[:, s], sems.at[k]))
        copies[-1].start()
    for c in copies:
        c.wait()


def run(kernel, outs, *args, cycles=None):
    whole = pl.BlockSpec(memory_space=VMEM)
    return pl.pallas_call(
        kernel,
        out_shape=[VMEM(shape, F32) if inside else jax.ShapeDtypeStruct(shape, F32) for shape, inside in outs],
        in_specs=[whole] * len(args),
        out_specs=[whole] * len(outs),
        compiler_params=pltpu.CompilerParams(vmem_limit_bytes=24 << 20),
    )(*[pltpu.with_memory_space_constraint(a, VMEM) for a in args])


def per_device(solution, incident, leaf_blocks, leaf_inverse, col_basis, row_basis):
    levels, rank, rows = row_basis.shape
    cols = solution.shape[0]
    dense = (packed_rows(cols, rank), LANES)
    in_field = ((cols, rows), True)
    low_out = ((levels - 1 - TOP, *dense), True)
    top_out = ((TOP, *dense), True)
    in_vmem = pl.BlockSpec(memory_space=VMEM)
    in_hbm = pl.BlockSpec(memory_space=pltpu.HBM)
    params = pltpu.CompilerParams(vmem_limit_bytes=24 << 20)
    top, field, row_basis = pl.pallas_call(
        first_top_kernel,
        out_shape=[VMEM(top_out[0], F32), VMEM(solution.shape, F32), VMEM(row_basis.shape, F32)],
        in_specs=[in_hbm] * 2,
        out_specs=[in_vmem] * 3,
        scratch_shapes=[pltpu.SemaphoreType.DMA((levels + 1,))],
        compiler_params=params,
    )(*[pltpu.with_memory_space_constraint(a, pltpu.HBM) for a in (solution, row_basis)])
    (low,) = run(low_kernel, [low_out], field, row_basis)

    def near_of(field):
        return run(near_kernel, [in_field], field, incident, leaf_blocks, col_basis, row_basis)

    def near_and_copy(field):
        outs = [in_field, ((cols, rows), False)]
        return run(near_and_copy_kernel, outs, field, incident, leaf_blocks, col_basis, row_basis)

    def apply(start, near, coefs):
        return run(functools.partial(apply_kernel, start), [in_field], near, coefs, col_basis)[0]

    near, start, coefs, _ = exchange(low, top, functools.partial(near_of, field), apply)
    refined, top = run(
        functools.partial(refine_kernel, start),
        [in_field, top_out],
        near,
        coefs,
        field,
        col_basis,
        leaf_inverse,
        row_basis,
    )
    (low,) = run(low_kernel, [low_out], refined, row_basis)
    near, start, coefs, others = exchange(low, top, functools.partial(near_and_copy, refined), apply)
    residual = pl.pallas_call(
        functools.partial(last_kernel, start),
        out_shape=jax.ShapeDtypeStruct((cols, rows), F32),
        in_specs=[in_vmem] * 3,
        out_specs=in_hbm,
        scratch_shapes=[VMEM((cols, rows), F32), pltpu.SemaphoreType.DMA((4,))],
        compiler_params=params,
    )(*[pltpu.with_memory_space_constraint(a, VMEM) for a in (near, coefs, col_basis)])
    return (others[0], residual)


def solution(mesh):
    in_specs = (
        P(None, ("wide", "grp")),
        P(None, ("wide", "grp")),
        P(None, ("wide", "grp")),
        P(None, ("wide", "grp")),
        P(None, None, ("wide", "grp")),
        P(None, None, ("wide", "grp")),
    )
    out_specs = (P(None, ("wide", "grp")), P(None, ("wide", "grp")))
    return jax.shard_map(
        per_device, mesh=mesh, in_specs=in_specs, out_specs=out_specs, check_vma=False
    )
```

```python
import functools

import jax
import jax.numpy as jnp
from jax import lax
from jax.experimental import pallas as pl
from jax.experimental.pallas import tpu as pltpu
from jax.sharding import PartitionSpec as P

AXES = ("wide", "grp")
LANES = 128
TOP = 2
VMEM = pltpu.VMEM
F32 = jnp.float32
ROWS_OF_BOTH = (((1,), (1,)), ((), ()))
PLAIN = (((1,), (0,)), ((), ()))


def bits_of(axis):
    return lax.axis_size(axis).bit_length() - 1


def parity(number):
    return number.bit_count() & 1


def swap(block, masks):
    wides, grps = lax.axis_size("wide"), lax.axis_size("grp")
    route = []
    for w in range(wides):
        for g in range(grps):
            wide_mask, grp_mask = masks[parity(w) ^ parity(g)]
            route.append((w * grps + g, (w ^ wide_mask) * grps + (g ^ grp_mask)))
    return lax.ppermute(block, AXES, route)


def both(wide_mask, grp_mask):
    return ((wide_mask, grp_mask), (wide_mask, grp_mask))


def climb_tree(low, top, near_of, apply):
    gathered = []
    pending = jnp.concatenate([low, top])
    masks = [both(0, 1 << b) for b in range(bits_of("grp"))]
    masks += [both(1 << b, 0) for b in range(bits_of("wide"))]
    for mask in masks:
        received = swap(pending, mask)
        gathered.append(received[0])
        pending = (pending + received)[1:]
    near, *others = near_of()
    near = apply(1, near, jnp.stack(gathered[:-TOP]))
    return near, 1 + len(gathered) - TOP, jnp.stack(gathered[-TOP:]), others


def in_first_lane():
    ones = lax.axis_index("wide") ^ lax.axis_index("grp")
    for shift in range(1, max(bits_of("wide"), bits_of("grp"))):
        ones ^= (lax.axis_index("wide") >> shift) ^ (lax.axis_index("grp") >> shift)
    return (ones & 1) == 0


def in_lanes(first, low, top, near_of, apply):
    core = both(1, 0)
    top = top + swap(top, core)
    next_low = swap(jnp.stack([low[0], low[2]]), both(0, 1))
    top = top + swap(top, both(1, 1))
    top, next_low = lax.optimization_barrier((top, next_low))
    near, *others = near_of()
    own = jnp.where(first, top[0], top[1])
    far_low = swap(low[1:], both(0, 2))
    last_low = swap(low[1:], both(0, 3))
    far = swap(own, ((2, 2), (4, 2)))
    corner = swap(top[1], ((6, 0), (7, 2)))
    own, far_low = lax.optimization_barrier((own, far_low))
    beside = swap(own, ((3, 0), (5, 0)))
    far_low, last_low, far, corner, beside = lax.optimization_barrier((far_low, last_low, far, corner, beside))
    both_low = far_low + last_low
    near = apply(1, near, jnp.stack([next_low[0], both_low[0]]))
    mine = beside + far
    third = low[2] + next_low[1] + both_low[1]
    third, other, corner_other = swap(jnp.stack([third, mine, corner]), core)
    fourth = jnp.where(first, mine, other)
    fifth = jnp.where(first, other, mine) + (corner + corner_other)
    return near, 3, jnp.stack([third, fourth, fifth]), others


def exchange(first, low, top, near_of, apply):
    if bits_of("grp") == 2 and bits_of("wide") == 3:
        return in_lanes(first, low, top, near_of, apply)
    return climb_tree(low, top, near_of, apply)


def split(x):
    high = x.astype(jnp.bfloat16)
    return high, (x - high.astype(F32)).astype(jnp.bfloat16)


def dot(x, table, dims):
    count = x.shape[0]
    x_high, x_low = split(x)
    t_high, t_low = split(table)
    main = lax.dot_general(jnp.concatenate([x_high, x_low]), t_high, dims, preferred_element_type=F32)
    rest = lax.dot_general(x_high, t_low, dims, preferred_element_type=F32)
    return main[:count] + (main[count:] + rest)


def merged(basis):
    return basis.reshape(-1, basis.shape[-1])


def chunks_of(rank):
    widths = [LANES] * (rank // LANES)
    return widths + [w for w in (1 << b for b in reversed(range(LANES.bit_length() - 1))) if rank % LANES & w]


def packed_rows(cols, rank):
    return cols * rank // LANES


def pack(block):
    cols, rank = block.shape
    out, at = [], 0
    for w in chunks_of(rank):
        rows = cols * w // LANES
        piece = block[:, at : at + w]
        out.append(jnp.concatenate([piece[r : r + rows] for r in range(0, cols, rows)], axis=1))
        at += w
    return jnp.concatenate(out)


def unpack(dense, cols):
    out, at = [], 0
    for w in chunks_of(dense.shape[0] * LANES // cols):
        rows = cols * w // LANES
        piece = dense[at : at + rows]
        out.append(jnp.concatenate([piece[:, l : l + w] for l in range(0, LANES, w)]))
        at += rows
    return jnp.concatenate(out, axis=1)


def side_by_side(coefs, cols):
    return jnp.concatenate([unpack(coefs[l], cols) for l in range(coefs.shape[0])], axis=1)


def store_levels(ref, wide_block):
    rank = wide_block.shape[1] // ref.shape[0]
    for l in range(ref.shape[0]):
        ref[l] = pack(wide_block[:, l * rank : (l + 1) * rank])


def leaf_slices(blocks):
    leaf, rows = blocks.shape
    return [slice(s, s + leaf) for s in range(0, rows, leaf)]


def near_kernel(field, incident, leaf_blocks, col_basis, row_basis, near):
    pieces = leaf_slices(leaf_blocks)
    coefs = [dot(field[:, s], row_basis[0, :, s], ROWS_OF_BOTH) for s in pieces]
    for k, s in enumerate(pieces):
        image = dot(field[:, s], leaf_blocks[:, s], PLAIN)
        near[:, s] = incident[:, s] - image - dot(coefs[k ^ 1], col_basis[0, :, s], PLAIN)


def near_and_copy_kernel(field, incident, leaf_blocks, col_basis, row_basis, near, copy):
    copy[...] = field[...]
    near_kernel(field, incident, leaf_blocks, col_basis, row_basis, near)


def first_top_kernel(field_hbm, row_hbm, top, field, row, sems):
    levels = row_hbm.shape[0]
    copies = [pltpu.make_async_copy(field_hbm, field, sems.at[levels])]
    copies += [pltpu.make_async_copy(row_hbm.at[l], row.at[l], sems.at[l]) for l in reversed(range(levels))]
    for c in copies:
        c.start()
    for c in copies[: TOP + 1]:
        c.wait()
    store_levels(top, dot(field[...], merged(row[levels - TOP :]), ROWS_OF_BOTH))
    for c in copies[TOP + 1 :]:
        c.wait()


def low_kernel(field, row_basis, low):
    store_levels(low, dot(field[...], merged(row_basis[1 : row_basis.shape[0] - TOP]), ROWS_OF_BOTH))


def apply_kernel(start, near, coefs, col_basis, out):
    table = merged(col_basis[start : start + coefs.shape[0]])
    out[...] = near[...] - dot(side_by_side(coefs, near.shape[0]), table, PLAIN)


def refine_kernel(start, near, coefs, field, col_basis, leaf_inverse, row_basis, refined, top):
    levels = col_basis.shape[0]
    table = merged(col_basis[start:])
    first = near[...] - dot(side_by_side(coefs, near.shape[0]), table, PLAIN)
    for s in leaf_slices(leaf_inverse):
        refined[:, s] = field[:, s] + dot(first[:, s], leaf_inverse[:, s], PLAIN)
    store_levels(top, dot(refined[...], merged(row_basis[levels - TOP :]), ROWS_OF_BOTH))


def last_kernel(start, near, coefs, col_basis, out_hbm, out, sems):
    coefs = side_by_side(coefs, near.shape[0])
    rows = near.shape[1]
    step = rows // sems.shape[0]
    copies = []
    for k in range(sems.shape[0]):
        s = slice(k * step, k * step + step)
        out[:, s] = near[:, s] - dot(coefs, merged(col_basis[start:, :, s]), PLAIN)
        copies.append(pltpu.make_async_copy(out.at[:, s], out_hbm.at[:, s], sems.at[k]))
        copies[-1].start()
    for c in copies:
        c.wait()


def run(kernel, outs, *args, cycles=None):
    whole = pl.BlockSpec(memory_space=VMEM)
    return pl.pallas_call(
        kernel,
        out_shape=[VMEM(shape, F32) if inside else jax.ShapeDtypeStruct(shape, F32) for shape, inside in outs],
        in_specs=[whole] * len(args),
        out_specs=[whole] * len(outs),
        compiler_params=pltpu.CompilerParams(vmem_limit_bytes=24 << 20),
    )(*[pltpu.with_memory_space_constraint(a, VMEM) for a in args])


def per_device(solution, incident, leaf_blocks, leaf_inverse, col_basis, row_basis):
    solution, first = lax.optimization_barrier((solution, in_first_lane()))
    levels, rank, rows = row_basis.shape
    cols = solution.shape[0]
    dense = (packed_rows(cols, rank), LANES)
    in_field = ((cols, rows), True)
    low_out = ((levels - 1 - TOP, *dense), True)
    top_out = ((TOP, *dense), True)
    in_vmem = pl.BlockSpec(memory_space=VMEM)
    in_hbm = pl.BlockSpec(memory_space=pltpu.HBM)
    params = pltpu.CompilerParams(vmem_limit_bytes=24 << 20)
    top, field, row_basis = pl.pallas_call(
        first_top_kernel,
        out_shape=[VMEM(top_out[0], F32), VMEM(solution.shape, F32), VMEM(row_basis.shape, F32)],
        in_specs=[in_hbm] * 2,
        out_specs=[in_vmem] * 3,
        scratch_shapes=[pltpu.SemaphoreType.DMA((levels + 1,))],
        compiler_params=params,
    )(*[pltpu.with_memory_space_constraint(a, pltpu.HBM) for a in (solution, row_basis)])
    (low,) = run(low_kernel, [low_out], field, row_basis)

    def near_of(field):
        return run(near_kernel, [in_field], field, incident, leaf_blocks, col_basis, row_basis)

    def near_and_copy(field):
        outs = [in_field, ((cols, rows), False)]
        return run(near_and_copy_kernel, outs, field, incident, leaf_blocks, col_basis, row_basis)

    def apply(start, near, coefs):
        return run(functools.partial(apply_kernel, start), [in_field], near, coefs, col_basis)[0]

    near, start, coefs, _ = exchange(first, low, top, functools.partial(near_of, field), apply)
    refined, top = run(
        functools.partial(refine_kernel, start),
        [in_field, top_out],
        near,
        coefs,
        field,
        col_basis,
        leaf_inverse,
        row_basis,
    )
    (low,) = run(low_kernel, [low_out], refined, row_basis)
    near, start, coefs, others = exchange(first, low, top, functools.partial(near_and_copy, refined), apply)
    residual = pl.pallas_call(
        functools.partial(last_kernel, start),
        out_shape=jax.ShapeDtypeStruct((cols, rows), F32),
        in_specs=[in_vmem] * 3,
        out_specs=in_hbm,
        scratch_shapes=[VMEM((cols, rows), F32), pltpu.SemaphoreType.DMA((4,))],
        compiler_params=params,
    )(*[pltpu.with_memory_space_constraint(a, VMEM) for a in (near, coefs, col_basis)])
    return (others[0], residual)


def solution(mesh):
    in_specs = (
        P(None, ("wide", "grp")),
        P(None, ("wide", "grp")),
        P(None, ("wide", "grp")),
        P(None, ("wide", "grp")),
        P(None, None, ("wide", "grp")),
        P(None, None, ("wide", "grp")),
    )
    out_specs = (P(None, ("wide", "grp")), P(None, ("wide", "grp")))
    return jax.shard_map(
        per_device, mesh=mesh, in_specs=in_specs, out_specs=out_specs, check_vma=False
    )
```

```python
import functools

import jax
import jax.numpy as jnp
from jax import lax
from jax.experimental import pallas as pl
from jax.experimental.pallas import tpu as pltpu
from jax.sharding import PartitionSpec as P

AXES = ("wide", "grp")
LANES = 128
TOP = 2
VMEM = pltpu.VMEM
F32 = jnp.float32
ROWS_OF_BOTH = (((1,), (1,)), ((), ()))
PLAIN = (((1,), (0,)), ((), ()))


def bits_of(axis):
    return lax.axis_size(axis).bit_length() - 1


def parity(number):
    return number.bit_count() & 1


def swap(block, masks):
    wides, grps = lax.axis_size("wide"), lax.axis_size("grp")
    route = []
    for w in range(wides):
        for g in range(grps):
            wide_mask, grp_mask = masks[parity(w) ^ parity(g)]
            route.append((w * grps + g, (w ^ wide_mask) * grps + (g ^ grp_mask)))
    return lax.ppermute(block, AXES, route)


def both(wide_mask, grp_mask):
    return ((wide_mask, grp_mask), (wide_mask, grp_mask))


def climb_tree(low, top, near_of, apply):
    gathered = []
    pending = jnp.concatenate([low, top])
    masks = [both(0, 1 << b) for b in range(bits_of("grp"))]
    masks += [both(1 << b, 0) for b in range(bits_of("wide"))]
    for mask in masks:
        received = swap(pending, mask)
        gathered.append(received[0])
        pending = (pending + received)[1:]
    near, *others = near_of()
    near = apply(1, near, jnp.stack(gathered[:-TOP]))
    return near, 1 + len(gathered) - TOP, jnp.stack(gathered[-TOP:]), others


def in_first_lane():
    ones = lax.axis_index("wide") ^ lax.axis_index("grp")
    for shift in range(1, max(bits_of("wide"), bits_of("grp"))):
        ones ^= (lax.axis_index("wide") >> shift) ^ (lax.axis_index("grp") >> shift)
    return (ones & 1) == 0


def in_lanes(first, low, top, near_of, apply):
    core = both(1, 0)
    top = top + swap(top, core)
    next_low = swap(jnp.stack([low[0], low[2]]), both(0, 1))
    top_got = swap(top, both(1, 1))
    top = top + top_got
    near, *others = near_of()
    top, next_low = lax.optimization_barrier((top, next_low))
    own = jnp.where(first, top[0], top[1])
    far_low = swap(low[1:], both(0, 2))
    last_low = swap(low[1:], both(0, 3))
    corner = swap(top[1], ((6, 0), (7, 2)))
    far = swap(own, ((2, 2), (4, 2)))
    own, last_low = lax.optimization_barrier((own, last_low))
    beside = swap(own, ((3, 0), (5, 0)))
    far_low, last_low, far, corner, beside = lax.optimization_barrier((far_low, last_low, far, corner, beside))
    both_low = far_low + last_low
    near = apply(1, near, jnp.stack([next_low[0], both_low[0]]))
    third = low[2] + next_low[1] + both_low[1]
    mine = beside + far
    third, other, corner_other = swap(jnp.stack([third, mine, corner]), core)
    fourth = jnp.where(first, mine, other)
    fifth = jnp.where(first, other, mine) + (corner + corner_other)
    return near, 3, jnp.stack([third, fourth, fifth]), others


def exchange(first, low, top, near_of, apply):
    if bits_of("grp") == 2 and bits_of("wide") == 3:
        return in_lanes(first, low, top, near_of, apply)
    return climb_tree(low, top, near_of, apply)


def split(x):
    high = x.astype(jnp.bfloat16)
    return high, (x - high.astype(F32)).astype(jnp.bfloat16)


def dot(x, table, dims):
    count = x.shape[0]
    x_high, x_low = split(x)
    t_high, t_low = split(table)
    main = lax.dot_general(jnp.concatenate([x_high, x_low]), t_high, dims, preferred_element_type=F32)
    rest = lax.dot_general(x_high, t_low, dims, preferred_element_type=F32)
    return main[:count] + (main[count:] + rest)


def merged(basis):
    return basis.reshape(-1, basis.shape[-1])


def chunks_of(rank):
    widths = [LANES] * (rank // LANES)
    return widths + [w for w in (1 << b for b in reversed(range(LANES.bit_length() - 1))) if rank % LANES & w]


def packed_rows(cols, rank):
    return cols * rank // LANES


def pack(block):
    cols, rank = block.shape
    out, at = [], 0
    for w in chunks_of(rank):
        rows = cols * w // LANES
        piece = block[:, at : at + w]
        out.append(jnp.concatenate([piece[r : r + rows] for r in range(0, cols, rows)], axis=1))
        at += w
    return jnp.concatenate(out)


def unpack(dense, cols):
    out, at = [], 0
    for w in chunks_of(dense.shape[0] * LANES // cols):
        rows = cols * w // LANES
        piece = dense[at : at + rows]
        out.append(jnp.concatenate([piece[:, l : l + w] for l in range(0, LANES, w)]))
        at += rows
    return jnp.concatenate(out, axis=1)


def side_by_side(coefs, cols):
    return jnp.concatenate([unpack(coefs[l], cols) for l in range(coefs.shape[0])], axis=1)


def store_levels(ref, wide_block):
    rank = wide_block.shape[1] // ref.shape[0]
    for l in range(ref.shape[0]):
        ref[l] = pack(wide_block[:, l * rank : (l + 1) * rank])


def leaf_slices(blocks):
    leaf, rows = blocks.shape
    return [slice(s, s + leaf) for s in range(0, rows, leaf)]


def near_kernel(field, incident, leaf_blocks, col_basis, row_basis, near):
    pieces = leaf_slices(leaf_blocks)
    coefs = [dot(field[:, s], row_basis[0, :, s], ROWS_OF_BOTH) for s in pieces]
    for k, s in enumerate(pieces):
        image = dot(field[:, s], leaf_blocks[:, s], PLAIN)
        near[:, s] = incident[:, s] - image - dot(coefs[k ^ 1], col_basis[0, :, s], PLAIN)


def near_and_copy_kernel(field, incident, leaf_blocks, col_basis, row_basis, near, copy):
    copy[...] = field[...]
    near_kernel(field, incident, leaf_blocks, col_basis, row_basis, near)


def first_top_kernel(field_hbm, row_hbm, top, field, row, sems):
    levels = row_hbm.shape[0]
    copies = [pltpu.make_async_copy(field_hbm, field, sems.at[levels])]
    copies += [pltpu.make_async_copy(row_hbm.at[l], row.at[l], sems.at[l]) for l in reversed(range(levels))]
    for c in copies:
        c.start()
    for c in copies[: TOP + 1]:
        c.wait()
    store_levels(top, dot(field[...], merged(row[levels - TOP :]), ROWS_OF_BOTH))
    for c in copies[TOP + 1 :]:
        c.wait()


def low_kernel(field, row_basis, low):
    store_levels(low, dot(field[...], merged(row_basis[1 : row_basis.shape[0] - TOP]), ROWS_OF_BOTH))


def apply_kernel(start, near, coefs, col_basis, out):
    table = merged(col_basis[start : start + coefs.shape[0]])
    out[...] = near[...] - dot(side_by_side(coefs, near.shape[0]), table, PLAIN)


def refine_kernel(start, near, coefs, field, col_basis, leaf_inverse, row_basis, refined, top):
    levels = col_basis.shape[0]
    table = merged(col_basis[start:])
    first = near[...] - dot(side_by_side(coefs, near.shape[0]), table, PLAIN)
    for s in leaf_slices(leaf_inverse):
        refined[:, s] = field[:, s] + dot(first[:, s], leaf_inverse[:, s], PLAIN)
    store_levels(top, dot(refined[...], merged(row_basis[levels - TOP :]), ROWS_OF_BOTH))


def last_kernel(start, near, coefs, col_basis, out_hbm, out, sems):
    coefs = side_by_side(coefs, near.shape[0])
    rows = near.shape[1]
    step = rows // sems.shape[0]
    copies = []
    for k in range(sems.shape[0]):
        s = slice(k * step, k * step + step)
        out[:, s] = near[:, s] - dot(coefs, merged(col_basis[start:, :, s]), PLAIN)
        copies.append(pltpu.make_async_copy(out.at[:, s], out_hbm.at[:, s], sems.at[k]))
        copies[-1].start()
    for c in copies:
        c.wait()


def run(kernel, outs, *args, cycles=None):
    whole = pl.BlockSpec(memory_space=VMEM)
    return pl.pallas_call(
        kernel,
        out_shape=[VMEM(shape, F32) if inside else jax.ShapeDtypeStruct(shape, F32) for shape, inside in outs],
        in_specs=[whole] * len(args),
        out_specs=[whole] * len(outs),
        compiler_params=pltpu.CompilerParams(vmem_limit_bytes=24 << 20),
    )(*[pltpu.with_memory_space_constraint(a, VMEM) for a in args])


def per_device(solution, incident, leaf_blocks, leaf_inverse, col_basis, row_basis):
    solution, first = lax.optimization_barrier((solution, in_first_lane()))
    levels, rank, rows = row_basis.shape
    cols = solution.shape[0]
    dense = (packed_rows(cols, rank), LANES)
    in_field = ((cols, rows), True)
    low_out = ((levels - 1 - TOP, *dense), True)
    top_out = ((TOP, *dense), True)
    in_vmem = pl.BlockSpec(memory_space=VMEM)
    in_hbm = pl.BlockSpec(memory_space=pltpu.HBM)
    params = pltpu.CompilerParams(vmem_limit_bytes=24 << 20)
    top, field, row_basis = pl.pallas_call(
        first_top_kernel,
        out_shape=[VMEM(top_out[0], F32), VMEM(solution.shape, F32), VMEM(row_basis.shape, F32)],
        in_specs=[in_hbm] * 2,
        out_specs=[in_vmem] * 3,
        scratch_shapes=[pltpu.SemaphoreType.DMA((levels + 1,))],
        compiler_params=params,
    )(*[pltpu.with_memory_space_constraint(a, pltpu.HBM) for a in (solution, row_basis)])
    (low,) = run(low_kernel, [low_out], field, row_basis)

    def near_of(field):
        return run(near_kernel, [in_field], field, incident, leaf_blocks, col_basis, row_basis)

    def near_and_copy(field):
        outs = [in_field, ((cols, rows), False)]
        return run(near_and_copy_kernel, outs, field, incident, leaf_blocks, col_basis, row_basis)

    def apply(start, near, coefs):
        return run(functools.partial(apply_kernel, start), [in_field], near, coefs, col_basis)[0]

    near, start, coefs, _ = exchange(first, low, top, functools.partial(near_of, field), apply)
    refined, top = run(
        functools.partial(refine_kernel, start),
        [in_field, top_out],
        near,
        coefs,
        field,
        col_basis,
        leaf_inverse,
        row_basis,
    )
    (low,) = run(low_kernel, [low_out], refined, row_basis)
    near, start, coefs, others = exchange(first, low, top, functools.partial(near_and_copy, refined), apply)
    residual = pl.pallas_call(
        functools.partial(last_kernel, start),
        out_shape=jax.ShapeDtypeStruct((cols, rows), F32),
        in_specs=[in_vmem] * 3,
        out_specs=in_hbm,
        scratch_shapes=[VMEM((cols, rows), F32), pltpu.SemaphoreType.DMA((4,))],
        compiler_params=params,
    )(*[pltpu.with_memory_space_constraint(a, VMEM) for a in (near, coefs, col_basis)])
    return (others[0], residual)


def solution(mesh):
    in_specs = (
        P(None, ("wide", "grp")),
        P(None, ("wide", "grp")),
        P(None, ("wide", "grp")),
        P(None, ("wide", "grp")),
        P(None, None, ("wide", "grp")),
        P(None, None, ("wide", "grp")),
    )
    out_specs = (P(None, ("wide", "grp")), P(None, ("wide", "grp")))
    return jax.shard_map(
        per_device, mesh=mesh, in_specs=in_specs, out_specs=out_specs, check_vma=False
    )
```

```python
import functools

import jax
import jax.numpy as jnp
from jax import lax
from jax.experimental import pallas as pl
from jax.experimental.pallas import tpu as pltpu
from jax.sharding import PartitionSpec as P

AXES = ("wide", "grp")
LANES = 128
TOP = 2
VMEM = pltpu.VMEM
F32 = jnp.float32
ROWS_OF_BOTH = (((1,), (1,)), ((), ()))
PLAIN = (((1,), (0,)), ((), ()))


def bits_of(axis):
    return lax.axis_size(axis).bit_length() - 1


def parity(number):
    return number.bit_count() & 1


def swap(block, masks):
    wides, grps = lax.axis_size("wide"), lax.axis_size("grp")
    route = []
    for w in range(wides):
        for g in range(grps):
            wide_mask, grp_mask = masks[parity(w) ^ parity(g)]
            route.append((w * grps + g, (w ^ wide_mask) * grps + (g ^ grp_mask)))
    return lax.ppermute(block, AXES, route)


def both(wide_mask, grp_mask):
    return ((wide_mask, grp_mask), (wide_mask, grp_mask))


def climb_tree(low, top, near_of, apply):
    gathered = []
    pending = jnp.concatenate([low, top])
    masks = [both(0, 1 << b) for b in range(bits_of("grp"))]
    masks += [both(1 << b, 0) for b in range(bits_of("wide"))]
    for mask in masks:
        received = swap(pending, mask)
        gathered.append(received[0])
        pending = (pending + received)[1:]
    near, *others = near_of()
    near = apply(1, near, jnp.stack(gathered[:-TOP]), *others)
    return near, 1 + len(gathered) - TOP, jnp.stack(gathered[-TOP:]), others


def in_first_lane():
    ones = lax.axis_index("wide") ^ lax.axis_index("grp")
    for shift in range(1, max(bits_of("wide"), bits_of("grp"))):
        ones ^= (lax.axis_index("wide") >> shift) ^ (lax.axis_index("grp") >> shift)
    return (ones & 1) == 0


def in_lanes(first, low, top, near_of, apply):
    core = both(1, 0)
    top = top + swap(top, core)
    next_low = swap(jnp.stack([low[0], low[2]]), both(0, 1))
    top_got = swap(top, both(1, 1))
    top = top + top_got
    near, *others = near_of()
    top, next_low = lax.optimization_barrier((top, next_low))
    own = jnp.where(first, top[0], top[1])
    far_low = swap(low[1:], both(0, 2))
    last_low = swap(low[1:], both(0, 3))
    corner = swap(top[1], ((6, 0), (7, 2)))
    far = swap(own, ((2, 2), (4, 2)))
    own, last_low = lax.optimization_barrier((own, last_low))
    beside = swap(own, ((3, 0), (5, 0)))
    far_low, last_low, far, corner, beside = lax.optimization_barrier((far_low, last_low, far, corner, beside))
    both_low = far_low + last_low
    near = apply(1, near, jnp.stack([next_low[0], both_low[0]]), *others)
    third = low[2] + next_low[1] + both_low[1]
    mine = beside + far
    third, other, corner_other = swap(jnp.stack([third, mine, corner]), core)
    fourth = jnp.where(first, mine, other)
    fifth = jnp.where(first, other, mine) + (corner + corner_other)
    return near, 3, jnp.stack([third, fourth, fifth]), others


def goes_in_lanes():
    return bits_of("grp") == 2 and bits_of("wide") == 3


def exchange(first, low, top, near_of, apply):
    if goes_in_lanes():
        return in_lanes(first, low, top, near_of, apply)
    return climb_tree(low, top, near_of, apply)


def split(x):
    high = x.astype(jnp.bfloat16)
    return high, (x - high.astype(F32)).astype(jnp.bfloat16)


def dot(x, table, dims):
    return dot_split(x, *split(table), dims)


def dot_split(x, t_high, t_low, dims):
    count = x.shape[0]
    x_high, x_low = split(x)
    main = lax.dot_general(jnp.concatenate([x_high, x_low]), t_high, dims, preferred_element_type=F32)
    rest = lax.dot_general(x_high, t_low, dims, preferred_element_type=F32)
    return main[:count] + (main[count:] + rest)


def merged(basis):
    return basis.reshape(-1, basis.shape[-1])


def chunks_of(rank):
    widths = [LANES] * (rank // LANES)
    return widths + [w for w in (1 << b for b in reversed(range(LANES.bit_length() - 1))) if rank % LANES & w]


def packed_rows(cols, rank):
    return cols * rank // LANES


def pack(block):
    cols, rank = block.shape
    out, at = [], 0
    for w in chunks_of(rank):
        rows = cols * w // LANES
        piece = block[:, at : at + w]
        out.append(jnp.concatenate([piece[r : r + rows] for r in range(0, cols, rows)], axis=1))
        at += w
    return jnp.concatenate(out)


def unpack(dense, cols):
    out, at = [], 0
    for w in chunks_of(dense.shape[0] * LANES // cols):
        rows = cols * w // LANES
        piece = dense[at : at + rows]
        out.append(jnp.concatenate([piece[:, l : l + w] for l in range(0, LANES, w)]))
        at += rows
    return jnp.concatenate(out, axis=1)


def side_by_side(coefs, cols):
    return jnp.concatenate([unpack(coefs[l], cols) for l in range(coefs.shape[0])], axis=1)


def store_levels(ref, wide_block):
    rank = wide_block.shape[1] // ref.shape[0]
    for l in range(ref.shape[0]):
        ref[l] = pack(wide_block[:, l * rank : (l + 1) * rank])


def leaf_slices(blocks):
    leaf, rows = blocks.shape
    return [slice(s, s + leaf) for s in range(0, rows, leaf)]


def near_kernel(field, incident, leaf_blocks, col_basis, row_basis, near):
    pieces = leaf_slices(leaf_blocks)
    coefs = [dot(field[:, s], row_basis[0, :, s], ROWS_OF_BOTH) for s in pieces]
    for k, s in enumerate(pieces):
        image = dot(field[:, s], leaf_blocks[:, s], PLAIN)
        near[:, s] = incident[:, s] - image - dot(coefs[k ^ 1], col_basis[0, :, s], PLAIN)


def near_and_copy_kernel(field, incident, leaf_blocks, col_basis, row_basis, near, copy):
    copy[...] = field[...]
    near_kernel(field, incident, leaf_blocks, col_basis, row_basis, near)


def first_top_kernel(field_hbm, row_hbm, top, field, row, sems):
    levels = row_hbm.shape[0]
    copies = [pltpu.make_async_copy(field_hbm, field, sems.at[levels])]
    copies += [pltpu.make_async_copy(row_hbm.at[l], row.at[l], sems.at[l]) for l in reversed(range(levels))]
    for c in copies:
        c.start()
    for c in copies[: TOP + 1]:
        c.wait()
    store_levels(top, dot(field[...], merged(row[levels - TOP :]), ROWS_OF_BOTH))
    for c in copies[TOP + 1 :]:
        c.wait()


def low_kernel(field, row_basis, low):
    store_levels(low, dot(field[...], merged(row_basis[1 : row_basis.shape[0] - TOP]), ROWS_OF_BOTH))


def apply_kernel(start, near, coefs, col_basis, out):
    table = merged(col_basis[start : start + coefs.shape[0]])
    out[...] = near[...] - dot(side_by_side(coefs, near.shape[0]), table, PLAIN)


def near_and_tables_kernel(
    start,
    field,
    incident,
    leaf_blocks,
    col_basis,
    row_basis,
    inverse_hbm,
    near,
    leaf_inverse,
    mixed_high,
    mixed_low,
    top_high,
    top_low,
    sem,
):
    copy = pltpu.make_async_copy(inverse_hbm, leaf_inverse, sem)
    copy.start()
    near_kernel(field, incident, leaf_blocks, col_basis, row_basis, near)
    copy.wait()
    for s in leaf_slices(leaf_inverse):
        mixed = dot(merged(col_basis[start:, :, s]), leaf_inverse[:, s], PLAIN)
        mixed_high[:, s], mixed_low[:, s] = split(mixed)
    top_high[...], top_low[...] = split(merged(row_basis[row_basis.shape[0] - TOP :]))


def apply_and_base_kernel(start, near, coefs, col_basis, field, leaf_inverse, base):
    table = merged(col_basis[start : start + coefs.shape[0]])
    first = near[...] - dot(side_by_side(coefs, near.shape[0]), table, PLAIN)
    for s in leaf_slices(leaf_inverse):
        base[:, s] = field[:, s] + dot(first[:, s], leaf_inverse[:, s], PLAIN)


def refine_kernel(base, coefs, mixed_high, mixed_low, top_high, top_low, refined, top):
    refined[...] = base[...] - dot_split(
        side_by_side(coefs, base.shape[0]), mixed_high[...], mixed_low[...], PLAIN
    )
    store_levels(top, dot_split(refined[...], top_high[...], top_low[...], ROWS_OF_BOTH))


def last_kernel(start, near, coefs, col_basis, out_hbm, out, sems):
    coefs = side_by_side(coefs, near.shape[0])
    rows = near.shape[1]
    step = rows // sems.shape[0]
    copies = []
    for k in range(sems.shape[0]):
        s = slice(k * step, k * step + step)
        out[:, s] = near[:, s] - dot(coefs, merged(col_basis[start:, :, s]), PLAIN)
        copies.append(pltpu.make_async_copy(out.at[:, s], out_hbm.at[:, s], sems.at[k]))
        copies[-1].start()
    for c in copies:
        c.wait()


def run(kernel, outs, *args, cycles=None):
    whole = pl.BlockSpec(memory_space=VMEM)
    return pl.pallas_call(
        kernel,
        out_shape=[VMEM(shape, kind) if inside else jax.ShapeDtypeStruct(shape, kind) for shape, inside, kind in outs],
        in_specs=[whole] * len(args),
        out_specs=[whole] * len(outs),
        compiler_params=pltpu.CompilerParams(vmem_limit_bytes=24 << 20),
    )(*[pltpu.with_memory_space_constraint(a, VMEM) for a in args])


def per_device(solution, incident, leaf_blocks, leaf_inverse, col_basis, row_basis):
    solution, first = lax.optimization_barrier((solution, in_first_lane()))
    levels, rank, rows = row_basis.shape
    cols = solution.shape[0]
    dense = (packed_rows(cols, rank), LANES)
    in_field = ((cols, rows), True, F32)
    low_out = ((levels - 1 - TOP, *dense), True, F32)
    top_out = ((TOP, *dense), True, F32)
    in_vmem = pl.BlockSpec(memory_space=VMEM)
    in_hbm = pl.BlockSpec(memory_space=pltpu.HBM)
    params = pltpu.CompilerParams(vmem_limit_bytes=24 << 20)
    top, field, row_basis = pl.pallas_call(
        first_top_kernel,
        out_shape=[VMEM(top_out[0], F32), VMEM(solution.shape, F32), VMEM(row_basis.shape, F32)],
        in_specs=[in_hbm] * 2,
        out_specs=[in_vmem] * 3,
        scratch_shapes=[pltpu.SemaphoreType.DMA((levels + 1,))],
        compiler_params=params,
    )(*[pltpu.with_memory_space_constraint(a, pltpu.HBM) for a in (solution, row_basis)])
    (low,) = run(low_kernel, [low_out], field, row_basis)

    late = 3 if goes_in_lanes() else levels - TOP
    mixed_out = (((levels - late) * rank, rows), True, jnp.bfloat16)
    split_out = ((TOP * rank, rows), True, jnp.bfloat16)

    def near_and_tables():
        outs = [in_field, (leaf_inverse.shape, True, F32), mixed_out, mixed_out, split_out, split_out]
        in_place = [pltpu.with_memory_space_constraint(a, VMEM) for a in (field, incident, leaf_blocks, col_basis, row_basis)]
        return pl.pallas_call(
            functools.partial(near_and_tables_kernel, late),
            out_shape=[VMEM(shape, kind) for shape, _, kind in outs],
            in_specs=[in_vmem] * 5 + [in_hbm],
            out_specs=[in_vmem] * len(outs),
            scratch_shapes=[pltpu.SemaphoreType.DMA],
            compiler_params=params,
        )(*in_place, pltpu.with_memory_space_constraint(leaf_inverse, pltpu.HBM))

    def apply_and_base(start, near, coefs, inverse, *_):
        kernel = functools.partial(apply_and_base_kernel, start)
        return run(kernel, [in_field], near, coefs, col_basis, field, inverse)[0]

    def near_and_copy():
        outs = [in_field, ((cols, rows), False, F32)]
        return run(near_and_copy_kernel, outs, refined, incident, leaf_blocks, col_basis, row_basis)

    def apply(start, near, coefs, *_):
        return run(functools.partial(apply_kernel, start), [in_field], near, coefs, col_basis)[0]

    base, start, coefs, tables = exchange(first, low, top, near_and_tables, apply_and_base)
    refined, top = run(refine_kernel, [in_field, top_out], base, coefs, *tables[1:])
    (low,) = run(low_kernel, [low_out], refined, row_basis)
    near, start, coefs, others = exchange(first, low, top, near_and_copy, apply)
    residual = pl.pallas_call(
        functools.partial(last_kernel, start),
        out_shape=jax.ShapeDtypeStruct((cols, rows), F32),
        in_specs=[in_vmem] * 3,
        out_specs=in_hbm,
        scratch_shapes=[VMEM((cols, rows), F32), pltpu.SemaphoreType.DMA((4,))],
        compiler_params=params,
    )(*[pltpu.with_memory_space_constraint(a, VMEM) for a in (near, coefs, col_basis)])
    return (others[0], residual)


def solution(mesh):
    in_specs = (
        P(None, ("wide", "grp")),
        P(None, ("wide", "grp")),
        P(None, ("wide", "grp")),
        P(None, ("wide", "grp")),
        P(None, None, ("wide", "grp")),
        P(None, None, ("wide", "grp")),
    )
    out_specs = (P(None, ("wide", "grp")), P(None, ("wide", "grp")))
    return jax.shard_map(
        per_device, mesh=mesh, in_specs=in_specs, out_specs=out_specs, check_vma=False
    )
```

```python
import functools

import jax
import jax.numpy as jnp
from jax import lax
from jax.experimental import pallas as pl
from jax.experimental.pallas import tpu as pltpu
from jax.sharding import PartitionSpec as P

AXES = ("wide", "grp")
LANES = 128
TOP = 2
VMEM = pltpu.VMEM
F32 = jnp.float32
ROWS_OF_BOTH = (((1,), (1,)), ((), ()))
PLAIN = (((1,), (0,)), ((), ()))


def bits_of(axis):
    return lax.axis_size(axis).bit_length() - 1


def parity(number):
    return number.bit_count() & 1


def swap(block, masks):
    wides, grps = lax.axis_size("wide"), lax.axis_size("grp")
    route = []
    for w in range(wides):
        for g in range(grps):
            wide_mask, grp_mask = masks[parity(w) ^ parity(g)]
            route.append((w * grps + g, (w ^ wide_mask) * grps + (g ^ grp_mask)))
    return lax.ppermute(block, AXES, route)


def both(wide_mask, grp_mask):
    return ((wide_mask, grp_mask), (wide_mask, grp_mask))


def climb_tree(low, top, near_of, apply):
    gathered = []
    pending = jnp.concatenate([low, top])
    masks = [both(0, 1 << b) for b in range(bits_of("grp"))]
    masks += [both(1 << b, 0) for b in range(bits_of("wide"))]
    for mask in masks:
        received = swap(pending, mask)
        gathered.append(received[0])
        pending = (pending + received)[1:]
    near, *others = near_of()
    near = apply(1, near, jnp.stack(gathered[:-TOP]), *others)
    return near, 1 + len(gathered) - TOP, jnp.stack(gathered[-TOP:]), others


def in_first_lane():
    ones = lax.axis_index("wide") ^ lax.axis_index("grp")
    for shift in range(1, max(bits_of("wide"), bits_of("grp"))):
        ones ^= (lax.axis_index("wide") >> shift) ^ (lax.axis_index("grp") >> shift)
    return (ones & 1) == 0


def in_lanes(first, low, top, near_of, apply):
    core = both(1, 0)
    top = top + swap(top, core)
    next_low = swap(jnp.stack([low[0], low[2]]), both(0, 1))
    top_got = swap(top, both(1, 1))
    top = top + top_got
    near, *others = near_of()
    top, next_low = lax.optimization_barrier((top, next_low))
    own = jnp.where(first, top[0], top[1])
    far_low = swap(low[1:], both(0, 2))
    last_low = swap(low[1:], both(0, 3))
    corner = swap(top[1], ((6, 0), (7, 2)))
    far = swap(own, ((2, 2), (4, 2)))
    own, last_low = lax.optimization_barrier((own, last_low))
    beside = swap(own, ((3, 0), (5, 0)))
    far_low, last_low = lax.optimization_barrier((far_low, last_low))
    both_low = far_low + last_low
    third = swap(low[2] + next_low[1] + both_low[1], core)
    far, corner, beside, third = lax.optimization_barrier((far, corner, beside, third))
    mine = beside + far
    other, corner_other = swap(jnp.stack([mine, corner]), core)
    near = apply(1, near, jnp.stack([next_low[0], both_low[0], third]), *others)
    fourth = jnp.where(first, mine, other)
    fifth = jnp.where(first, other, mine) + (corner + corner_other)
    return near, 4, jnp.stack([fourth, fifth]), others


def goes_in_lanes():
    return bits_of("grp") == 2 and bits_of("wide") == 3


def exchange(first, low, top, near_of, apply):
    if goes_in_lanes():
        return in_lanes(first, low, top, near_of, apply)
    return climb_tree(low, top, near_of, apply)


def split(x):
    high = x.astype(jnp.bfloat16)
    return high, (x - high.astype(F32)).astype(jnp.bfloat16)


def dot(x, table, dims):
    return dot_split(x, *split(table), dims)


def dot_split(x, t_high, t_low, dims):
    count = x.shape[0]
    x_high, x_low = split(x)
    main = lax.dot_general(jnp.concatenate([x_high, x_low]), t_high, dims, preferred_element_type=F32)
    rest = lax.dot_general(x_high, t_low, dims, preferred_element_type=F32)
    return main[:count] + (main[count:] + rest)


def merged(basis):
    return basis.reshape(-1, basis.shape[-1])


def chunks_of(rank):
    widths = [LANES] * (rank // LANES)
    return widths + [w for w in (1 << b for b in reversed(range(LANES.bit_length() - 1))) if rank % LANES & w]


def packed_rows(cols, rank):
    return cols * rank // LANES


def pack(block):
    cols, rank = block.shape
    out, at = [], 0
    for w in chunks_of(rank):
        rows = cols * w // LANES
        piece = block[:, at : at + w]
        out.append(jnp.concatenate([piece[r : r + rows] for r in range(0, cols, rows)], axis=1))
        at += w
    return jnp.concatenate(out)


def unpack(dense, cols):
    out, at = [], 0
    for w in chunks_of(dense.shape[0] * LANES // cols):
        rows = cols * w // LANES
        piece = dense[at : at + rows]
        out.append(jnp.concatenate([piece[:, l : l + w] for l in range(0, LANES, w)]))
        at += rows
    return jnp.concatenate(out, axis=1)


def side_by_side(coefs, cols):
    return jnp.concatenate([unpack(coefs[l], cols) for l in range(coefs.shape[0])], axis=1)


def store_levels(ref, wide_block):
    rank = wide_block.shape[1] // ref.shape[0]
    for l in range(ref.shape[0]):
        ref[l] = pack(wide_block[:, l * rank : (l + 1) * rank])


def leaf_slices(blocks):
    leaf, rows = blocks.shape
    return [slice(s, s + leaf) for s in range(0, rows, leaf)]


def near_kernel(field, incident, leaf_blocks, col_basis, row_basis, near):
    pieces = leaf_slices(leaf_blocks)
    coefs = [dot(field[:, s], row_basis[0, :, s], ROWS_OF_BOTH) for s in pieces]
    for k, s in enumerate(pieces):
        image = dot(field[:, s], leaf_blocks[:, s], PLAIN)
        near[:, s] = incident[:, s] - image - dot(coefs[k ^ 1], col_basis[0, :, s], PLAIN)


def near_and_copy_kernel(field, incident, leaf_blocks, col_basis, row_basis, near, copy):
    copy[...] = field[...]
    near_kernel(field, incident, leaf_blocks, col_basis, row_basis, near)


def first_top_kernel(field_hbm, row_hbm, top, field, row, sems):
    levels = row_hbm.shape[0]
    copies = [pltpu.make_async_copy(field_hbm, field, sems.at[levels])]
    copies += [pltpu.make_async_copy(row_hbm.at[l], row.at[l], sems.at[l]) for l in reversed(range(levels))]
    for c in copies:
        c.start()
    for c in copies[: TOP + 1]:
        c.wait()
    store_levels(top, dot(field[...], merged(row[levels - TOP :]), ROWS_OF_BOTH))
    for c in copies[TOP + 1 :]:
        c.wait()


def low_kernel(field, row_basis, low):
    store_levels(low, dot(field[...], merged(row_basis[1 : row_basis.shape[0] - TOP]), ROWS_OF_BOTH))


def apply_kernel(start, near, coefs, col_basis, out):
    table = merged(col_basis[start : start + coefs.shape[0]])
    out[...] = near[...] - dot(side_by_side(coefs, near.shape[0]), table, PLAIN)


def near_and_tables_kernel(
    start,
    field,
    incident,
    leaf_blocks,
    col_basis,
    row_basis,
    inverse_hbm,
    near,
    leaf_inverse,
    mixed_high,
    mixed_low,
    top_high,
    top_low,
    sem,
):
    copy = pltpu.make_async_copy(inverse_hbm, leaf_inverse, sem)
    copy.start()
    near_kernel(field, incident, leaf_blocks, col_basis, row_basis, near)
    copy.wait()
    for s in leaf_slices(leaf_inverse):
        mixed = dot(merged(col_basis[start:, :, s]), leaf_inverse[:, s], PLAIN)
        mixed_high[:, s], mixed_low[:, s] = split(mixed)
    top_high[...], top_low[...] = split(merged(row_basis[row_basis.shape[0] - TOP :]))


def apply_and_base_kernel(start, near, coefs, col_basis, field, leaf_inverse, base):
    table = merged(col_basis[start : start + coefs.shape[0]])
    first = near[...] - dot(side_by_side(coefs, near.shape[0]), table, PLAIN)
    for s in leaf_slices(leaf_inverse):
        base[:, s] = field[:, s] + dot(first[:, s], leaf_inverse[:, s], PLAIN)


def refine_kernel(base, coefs, mixed_high, mixed_low, top_high, top_low, refined, top):
    refined[...] = base[...] - dot_split(
        side_by_side(coefs, base.shape[0]), mixed_high[...], mixed_low[...], PLAIN
    )
    store_levels(top, dot_split(refined[...], top_high[...], top_low[...], ROWS_OF_BOTH))


def last_kernel(start, near, coefs, col_basis, out_hbm, out, sems):
    coefs = side_by_side(coefs, near.shape[0])
    rows = near.shape[1]
    step = rows // sems.shape[0]
    copies = []
    for k in range(sems.shape[0]):
        s = slice(k * step, k * step + step)
        out[:, s] = near[:, s] - dot(coefs, merged(col_basis[start:, :, s]), PLAIN)
        copies.append(pltpu.make_async_copy(out.at[:, s], out_hbm.at[:, s], sems.at[k]))
        copies[-1].start()
    for c in copies:
        c.wait()


def run(kernel, outs, *args, cycles=None):
    whole = pl.BlockSpec(memory_space=VMEM)
    return pl.pallas_call(
        kernel,
        out_shape=[VMEM(shape, kind) if inside else jax.ShapeDtypeStruct(shape, kind) for shape, inside, kind in outs],
        in_specs=[whole] * len(args),
        out_specs=[whole] * len(outs),
        compiler_params=pltpu.CompilerParams(vmem_limit_bytes=24 << 20),
    )(*[pltpu.with_memory_space_constraint(a, VMEM) for a in args])


def per_device(solution, incident, leaf_blocks, leaf_inverse, col_basis, row_basis):
    solution, first = lax.optimization_barrier((solution, in_first_lane()))
    levels, rank, rows = row_basis.shape
    cols = solution.shape[0]
    dense = (packed_rows(cols, rank), LANES)
    in_field = ((cols, rows), True, F32)
    low_out = ((levels - 1 - TOP, *dense), True, F32)
    top_out = ((TOP, *dense), True, F32)
    in_vmem = pl.BlockSpec(memory_space=VMEM)
    in_hbm = pl.BlockSpec(memory_space=pltpu.HBM)
    params = pltpu.CompilerParams(vmem_limit_bytes=24 << 20)
    top, field, row_basis = pl.pallas_call(
        first_top_kernel,
        out_shape=[VMEM(top_out[0], F32), VMEM(solution.shape, F32), VMEM(row_basis.shape, F32)],
        in_specs=[in_hbm] * 2,
        out_specs=[in_vmem] * 3,
        scratch_shapes=[pltpu.SemaphoreType.DMA((levels + 1,))],
        compiler_params=params,
    )(*[pltpu.with_memory_space_constraint(a, pltpu.HBM) for a in (solution, row_basis)])
    (low,) = run(low_kernel, [low_out], field, row_basis)

    late = levels - TOP
    mixed_out = (((levels - late) * rank, rows), True, jnp.bfloat16)
    split_out = ((TOP * rank, rows), True, jnp.bfloat16)

    def near_and_tables():
        outs = [in_field, (leaf_inverse.shape, True, F32), mixed_out, mixed_out, split_out, split_out]
        in_place = [pltpu.with_memory_space_constraint(a, VMEM) for a in (field, incident, leaf_blocks, col_basis, row_basis)]
        return pl.pallas_call(
            functools.partial(near_and_tables_kernel, late),
            out_shape=[VMEM(shape, kind) for shape, _, kind in outs],
            in_specs=[in_vmem] * 5 + [in_hbm],
            out_specs=[in_vmem] * len(outs),
            scratch_shapes=[pltpu.SemaphoreType.DMA],
            compiler_params=params,
        )(*in_place, pltpu.with_memory_space_constraint(leaf_inverse, pltpu.HBM))

    def apply_and_base(start, near, coefs, inverse, *_):
        kernel = functools.partial(apply_and_base_kernel, start)
        return run(kernel, [in_field], near, coefs, col_basis, field, inverse)[0]

    def near_and_copy():
        outs = [in_field, ((cols, rows), False, F32)]
        return run(near_and_copy_kernel, outs, refined, incident, leaf_blocks, col_basis, row_basis)

    def apply(start, near, coefs, *_):
        return run(functools.partial(apply_kernel, start), [in_field], near, coefs, col_basis)[0]

    base, start, coefs, tables = exchange(first, low, top, near_and_tables, apply_and_base)
    refined, top = run(refine_kernel, [in_field, top_out], base, coefs, *tables[1:])
    (low,) = run(low_kernel, [low_out], refined, row_basis)
    near, start, coefs, others = exchange(first, low, top, near_and_copy, apply)
    residual = pl.pallas_call(
        functools.partial(last_kernel, start),
        out_shape=jax.ShapeDtypeStruct((cols, rows), F32),
        in_specs=[in_vmem] * 3,
        out_specs=in_hbm,
        scratch_shapes=[VMEM((cols, rows), F32), pltpu.SemaphoreType.DMA((4,))],
        compiler_params=params,
    )(*[pltpu.with_memory_space_constraint(a, VMEM) for a in (near, coefs, col_basis)])
    return (others[0], residual)


def solution(mesh):
    in_specs = (
        P(None, ("wide", "grp")),
        P(None, ("wide", "grp")),
        P(None, ("wide", "grp")),
        P(None, ("wide", "grp")),
        P(None, None, ("wide", "grp")),
        P(None, None, ("wide", "grp")),
    )
    out_specs = (P(None, ("wide", "grp")), P(None, ("wide", "grp")))
    return jax.shard_map(
        per_device, mesh=mesh, in_specs=in_specs, out_specs=out_specs, check_vma=False
    )
```

```python
import functools

import jax
import jax.numpy as jnp
from jax import lax
from jax.experimental import pallas as pl
from jax.experimental.pallas import tpu as pltpu
from jax.sharding import PartitionSpec as P

AXES = ("wide", "grp")
LANES = 128
TOP = 2
VMEM = pltpu.VMEM
F32 = jnp.float32
ROWS_OF_BOTH = (((1,), (1,)), ((), ()))
PLAIN = (((1,), (0,)), ((), ()))


def bits_of(axis):
    return lax.axis_size(axis).bit_length() - 1


def parity(number):
    return number.bit_count() & 1


def swap(block, masks):
    wides, grps = lax.axis_size("wide"), lax.axis_size("grp")
    route = []
    for w in range(wides):
        for g in range(grps):
            wide_mask, grp_mask = masks[parity(w) ^ parity(g)]
            route.append((w * grps + g, (w ^ wide_mask) * grps + (g ^ grp_mask)))
    return lax.ppermute(block, AXES, route)


def both(wide_mask, grp_mask):
    return ((wide_mask, grp_mask), (wide_mask, grp_mask))


def climb_tree(low, top, near_of, apply):
    gathered = []
    pending = jnp.concatenate([low, top])
    masks = [both(0, 1 << b) for b in range(bits_of("grp"))]
    masks += [both(1 << b, 0) for b in range(bits_of("wide"))]
    for mask in masks:
        received = swap(pending, mask)
        gathered.append(received[0])
        pending = (pending + received)[1:]
    near, *others = near_of()
    near = apply(1, near, jnp.stack(gathered[:-TOP]), *others)
    return near, 1 + len(gathered) - TOP, jnp.stack(gathered[-TOP:]), others


def in_first_lane():
    ones = lax.axis_index("wide") ^ lax.axis_index("grp")
    for shift in range(1, max(bits_of("wide"), bits_of("grp"))):
        ones ^= (lax.axis_index("wide") >> shift) ^ (lax.axis_index("grp") >> shift)
    return (ones & 1) == 0


def in_lanes(first, low, top, near_of, apply):
    core = both(1, 0)
    top = top + swap(top, core)
    next_low = swap(jnp.stack([low[0], low[2]]), both(0, 1))
    top_got = swap(top, both(1, 1))
    top = top + top_got
    near, *others = near_of()
    top, next_low = lax.optimization_barrier((top, next_low))
    own = jnp.where(first, top[0], top[1])
    far_low = swap(low[1:], both(0, 2))
    last_low = swap(low[1:], both(0, 3))
    corner = swap(top[1], ((7, 2), (6, 0)))
    far = swap(own, ((2, 2), (4, 2)))
    own, last_low = lax.optimization_barrier((own, last_low))
    beside = swap(own, ((3, 0), (5, 0)))
    far_low, last_low = lax.optimization_barrier((far_low, last_low))
    both_low = far_low + last_low
    third = swap(low[2] + next_low[1] + both_low[1], core)
    far, corner, beside, third = lax.optimization_barrier((far, corner, beside, third))
    mine = beside + far
    other, corner_other = swap(jnp.stack([mine, corner]), core)
    near = apply(1, near, jnp.stack([next_low[0], both_low[0], third]), *others)
    fourth = jnp.where(first, mine, other)
    fifth = jnp.where(first, other, mine) + (corner + corner_other)
    return near, 4, jnp.stack([fourth, fifth]), others


def goes_in_lanes():
    return bits_of("grp") == 2 and bits_of("wide") == 3


def exchange(first, low, top, near_of, apply):
    if goes_in_lanes():
        return in_lanes(first, low, top, near_of, apply)
    return climb_tree(low, top, near_of, apply)


def split(x):
    high = x.astype(jnp.bfloat16)
    return high, (x - high.astype(F32)).astype(jnp.bfloat16)


def dot(x, table, dims):
    return dot_split(x, *split(table), dims)


def dot_split(x, t_high, t_low, dims):
    count = x.shape[0]
    x_high, x_low = split(x)
    main = lax.dot_general(jnp.concatenate([x_high, x_low]), t_high, dims, preferred_element_type=F32)
    rest = lax.dot_general(x_high, t_low, dims, preferred_element_type=F32)
    return main[:count] + (main[count:] + rest)


def merged(basis):
    return basis.reshape(-1, basis.shape[-1])


def chunks_of(rank):
    widths = [LANES] * (rank // LANES)
    return widths + [w for w in (1 << b for b in reversed(range(LANES.bit_length() - 1))) if rank % LANES & w]


def packed_rows(cols, rank):
    return cols * rank // LANES


def pack(block):
    cols, rank = block.shape
    out, at = [], 0
    for w in chunks_of(rank):
        rows = cols * w // LANES
        piece = block[:, at : at + w]
        out.append(jnp.concatenate([piece[r : r + rows] for r in range(0, cols, rows)], axis=1))
        at += w
    return jnp.concatenate(out)


def unpack(dense, cols):
    out, at = [], 0
    for w in chunks_of(dense.shape[0] * LANES // cols):
        rows = cols * w // LANES
        piece = dense[at : at + rows]
        out.append(jnp.concatenate([piece[:, l : l + w] for l in range(0, LANES, w)]))
        at += rows
    return jnp.concatenate(out, axis=1)


def side_by_side(coefs, cols):
    return jnp.concatenate([unpack(coefs[l], cols) for l in range(coefs.shape[0])], axis=1)


def store_levels(ref, wide_block):
    rank = wide_block.shape[1] // ref.shape[0]
    for l in range(ref.shape[0]):
        ref[l] = pack(wide_block[:, l * rank : (l + 1) * rank])


def leaf_slices(blocks):
    leaf, rows = blocks.shape
    return [slice(s, s + leaf) for s in range(0, rows, leaf)]


def near_kernel(field, incident, leaf_blocks, col_basis, row_basis, near):
    pieces = leaf_slices(leaf_blocks)
    coefs = [dot(field[:, s], row_basis[0, :, s], ROWS_OF_BOTH) for s in pieces]
    for k, s in enumerate(pieces):
        image = dot(field[:, s], leaf_blocks[:, s], PLAIN)
        near[:, s] = incident[:, s] - image - dot(coefs[k ^ 1], col_basis[0, :, s], PLAIN)


def near_and_copy_kernel(field, incident, leaf_blocks, col_basis, row_basis, near, copy):
    copy[...] = field[...]
    near_kernel(field, incident, leaf_blocks, col_basis, row_basis, near)


def first_top_kernel(field_hbm, row_hbm, top, field, row, sems):
    levels = row_hbm.shape[0]
    copies = [pltpu.make_async_copy(field_hbm, field, sems.at[levels])]
    copies += [pltpu.make_async_copy(row_hbm.at[l], row.at[l], sems.at[l]) for l in reversed(range(levels))]
    for c in copies:
        c.start()
    for c in copies[: TOP + 1]:
        c.wait()
    store_levels(top, dot(field[...], merged(row[levels - TOP :]), ROWS_OF_BOTH))
    for c in copies[TOP + 1 :]:
        c.wait()


def low_kernel(field, row_basis, low):
    store_levels(low, dot(field[...], merged(row_basis[1 : row_basis.shape[0] - TOP]), ROWS_OF_BOTH))


def apply_kernel(start, near, coefs, col_basis, out):
    table = merged(col_basis[start : start + coefs.shape[0]])
    out[...] = near[...] - dot(side_by_side(coefs, near.shape[0]), table, PLAIN)


def near_and_tables_kernel(
    start,
    field,
    incident,
    leaf_blocks,
    col_basis,
    row_basis,
    inverse_hbm,
    near,
    leaf_inverse,
    mixed_high,
    mixed_low,
    top_high,
    top_low,
    sem,
):
    copy = pltpu.make_async_copy(inverse_hbm, leaf_inverse, sem)
    copy.start()
    near_kernel(field, incident, leaf_blocks, col_basis, row_basis, near)
    copy.wait()
    for s in leaf_slices(leaf_inverse):
        mixed = dot(merged(col_basis[start:, :, s]), leaf_inverse[:, s], PLAIN)
        mixed_high[:, s], mixed_low[:, s] = split(mixed)
    top_high[...], top_low[...] = split(merged(row_basis[row_basis.shape[0] - TOP :]))


def apply_and_base_kernel(start, near, coefs, col_basis, field, leaf_inverse, base):
    table = merged(col_basis[start : start + coefs.shape[0]])
    first = near[...] - dot(side_by_side(coefs, near.shape[0]), table, PLAIN)
    for s in leaf_slices(leaf_inverse):
        base[:, s] = field[:, s] + dot(first[:, s], leaf_inverse[:, s], PLAIN)


def refine_kernel(base, coefs, mixed_high, mixed_low, top_high, top_low, refined, top):
    refined[...] = base[...] - dot_split(
        side_by_side(coefs, base.shape[0]), mixed_high[...], mixed_low[...], PLAIN
    )
    store_levels(top, dot_split(refined[...], top_high[...], top_low[...], ROWS_OF_BOTH))


def last_kernel(start, near, coefs, col_basis, out_hbm, out, sems):
    coefs = side_by_side(coefs, near.shape[0])
    rows = near.shape[1]
    step = rows // sems.shape[0]
    copies = []
    for k in range(sems.shape[0]):
        s = slice(k * step, k * step + step)
        out[:, s] = near[:, s] - dot(coefs, merged(col_basis[start:, :, s]), PLAIN)
        copies.append(pltpu.make_async_copy(out.at[:, s], out_hbm.at[:, s], sems.at[k]))
        copies[-1].start()
    for c in copies:
        c.wait()


def run(kernel, outs, *args, cycles=None):
    whole = pl.BlockSpec(memory_space=VMEM)
    return pl.pallas_call(
        kernel,
        out_shape=[VMEM(shape, kind) if inside else jax.ShapeDtypeStruct(shape, kind) for shape, inside, kind in outs],
        in_specs=[whole] * len(args),
        out_specs=[whole] * len(outs),
        compiler_params=pltpu.CompilerParams(vmem_limit_bytes=24 << 20),
    )(*[pltpu.with_memory_space_constraint(a, VMEM) for a in args])


def per_device(solution, incident, leaf_blocks, leaf_inverse, col_basis, row_basis):
    solution, first = lax.optimization_barrier((solution, in_first_lane()))
    levels, rank, rows = row_basis.shape
    cols = solution.shape[0]
    dense = (packed_rows(cols, rank), LANES)
    in_field = ((cols, rows), True, F32)
    low_out = ((levels - 1 - TOP, *dense), True, F32)
    top_out = ((TOP, *dense), True, F32)
    in_vmem = pl.BlockSpec(memory_space=VMEM)
    in_hbm = pl.BlockSpec(memory_space=pltpu.HBM)
    params = pltpu.CompilerParams(vmem_limit_bytes=24 << 20)
    top, field, row_basis = pl.pallas_call(
        first_top_kernel,
        out_shape=[VMEM(top_out[0], F32), VMEM(solution.shape, F32), VMEM(row_basis.shape, F32)],
        in_specs=[in_hbm] * 2,
        out_specs=[in_vmem] * 3,
        scratch_shapes=[pltpu.SemaphoreType.DMA((levels + 1,))],
        compiler_params=params,
    )(*[pltpu.with_memory_space_constraint(a, pltpu.HBM) for a in (solution, row_basis)])
    (low,) = run(low_kernel, [low_out], field, row_basis)

    late = levels - TOP
    mixed_out = (((levels - late) * rank, rows), True, jnp.bfloat16)
    split_out = ((TOP * rank, rows), True, jnp.bfloat16)

    def near_and_tables():
        outs = [in_field, (leaf_inverse.shape, True, F32), mixed_out, mixed_out, split_out, split_out]
        in_place = [pltpu.with_memory_space_constraint(a, VMEM) for a in (field, incident, leaf_blocks, col_basis, row_basis)]
        return pl.pallas_call(
            functools.partial(near_and_tables_kernel, late),
            out_shape=[VMEM(shape, kind) for shape, _, kind in outs],
            in_specs=[in_vmem] * 5 + [in_hbm],
            out_specs=[in_vmem] * len(outs),
            scratch_shapes=[pltpu.SemaphoreType.DMA],
            compiler_params=params,
        )(*in_place, pltpu.with_memory_space_constraint(leaf_inverse, pltpu.HBM))

    def apply_and_base(start, near, coefs, inverse, *_):
        kernel = functools.partial(apply_and_base_kernel, start)
        return run(kernel, [in_field], near, coefs, col_basis, field, inverse)[0]

    def near_and_copy():
        outs = [in_field, ((cols, rows), False, F32)]
        return run(near_and_copy_kernel, outs, refined, incident, leaf_blocks, col_basis, row_basis)

    def apply(start, near, coefs, *_):
        return run(functools.partial(apply_kernel, start), [in_field], near, coefs, col_basis)[0]

    base, start, coefs, tables = exchange(first, low, top, near_and_tables, apply_and_base)
    refined, top = run(refine_kernel, [in_field, top_out], base, coefs, *tables[1:])
    (low,) = run(low_kernel, [low_out], refined, row_basis)
    near, start, coefs, others = exchange(first, low, top, near_and_copy, apply)
    residual = pl.pallas_call(
        functools.partial(last_kernel, start),
        out_shape=jax.ShapeDtypeStruct((cols, rows), F32),
        in_specs=[in_vmem] * 3,
        out_specs=in_hbm,
        scratch_shapes=[VMEM((cols, rows), F32), pltpu.SemaphoreType.DMA((4,))],
        compiler_params=params,
    )(*[pltpu.with_memory_space_constraint(a, VMEM) for a in (near, coefs, col_basis)])
    return (others[0], residual)


def solution(mesh):
    in_specs = (
        P(None, ("wide", "grp")),
        P(None, ("wide", "grp")),
        P(None, ("wide", "grp")),
        P(None, ("wide", "grp")),
        P(None, None, ("wide", "grp")),
        P(None, None, ("wide", "grp")),
    )
    out_specs = (P(None, ("wide", "grp")), P(None, ("wide", "grp")))
    return jax.shard_map(
        per_device, mesh=mesh, in_specs=in_specs, out_specs=out_specs, check_vma=False
    )
```

```python
import functools

import jax
import jax.numpy as jnp
from jax import lax
from jax.experimental import pallas as pl
from jax.experimental.pallas import tpu as pltpu
from jax.sharding import PartitionSpec as P

AXES = ("wide", "grp")
LANES = 128
TOP = 2
VMEM = pltpu.VMEM
F32 = jnp.float32
ROWS_OF_BOTH = (((1,), (1,)), ((), ()))
PLAIN = (((1,), (0,)), ((), ()))


def bits_of(axis):
    return lax.axis_size(axis).bit_length() - 1


def parity(number):
    return number.bit_count() & 1


def swap(block, masks):
    wides, grps = lax.axis_size("wide"), lax.axis_size("grp")
    route = []
    for w in range(wides):
        for g in range(grps):
            wide_mask, grp_mask = masks[parity(w) ^ parity(g)]
            route.append((w * grps + g, (w ^ wide_mask) * grps + (g ^ grp_mask)))
    return lax.ppermute(block, AXES, route)


def both(wide_mask, grp_mask):
    return ((wide_mask, grp_mask), (wide_mask, grp_mask))


def climb_tree(low, top, near_of, apply):
    gathered = []
    pending = jnp.concatenate([low, top])
    masks = [both(0, 1 << b) for b in range(bits_of("grp"))]
    masks += [both(1 << b, 0) for b in range(bits_of("wide"))]
    for mask in masks:
        received = swap(pending, mask)
        gathered.append(received[0])
        pending = (pending + received)[1:]
    near, *others = near_of()
    near = apply(1, near, jnp.stack(gathered[:-TOP]), *others)
    return near, 1 + len(gathered) - TOP, jnp.stack(gathered[-TOP:]), others


def in_first_lane():
    ones = lax.axis_index("wide") ^ lax.axis_index("grp")
    for shift in range(1, max(bits_of("wide"), bits_of("grp"))):
        ones ^= (lax.axis_index("wide") >> shift) ^ (lax.axis_index("grp") >> shift)
    return (ones & 1) == 0


def in_lanes(first, low, top, near_of, apply):
    core = both(1, 0)
    top = top + swap(top, core)
    next_low = swap(jnp.stack([low[0], low[2]]), both(0, 1))
    top_got = swap(top, both(0, 1))
    top = top + top_got
    near, *others = near_of()
    top, next_low = lax.optimization_barrier((top, next_low))
    own = jnp.where(first, top[0], top[1])
    far_low = swap(low[1:], both(0, 2))
    last_low = swap(low[1:], both(0, 3))
    corner = swap(top[1], ((7, 2), (6, 0)))
    far = swap(own, ((2, 2), (4, 2)))
    own, last_low = lax.optimization_barrier((own, last_low))
    beside = swap(own, ((3, 0), (5, 0)))
    far_low, last_low = lax.optimization_barrier((far_low, last_low))
    both_low = far_low + last_low
    third = swap(low[2] + next_low[1] + both_low[1], core)
    far, corner, beside, third = lax.optimization_barrier((far, corner, beside, third))
    mine = beside + far
    other, corner_other = swap(jnp.stack([mine, corner]), core)
    near = apply(1, near, jnp.stack([next_low[0], both_low[0], third]), *others)
    fourth = jnp.where(first, mine, other)
    fifth = jnp.where(first, other, mine) + (corner + corner_other)
    return near, 4, jnp.stack([fourth, fifth]), others


def goes_in_lanes():
    return bits_of("grp") == 2 and bits_of("wide") == 3


def exchange(first, low, top, near_of, apply):
    if goes_in_lanes():
        return in_lanes(first, low, top, near_of, apply)
    return climb_tree(low, top, near_of, apply)


def split(x):
    high = x.astype(jnp.bfloat16)
    return high, (x - high.astype(F32)).astype(jnp.bfloat16)


def dot(x, table, dims):
    return dot_split(x, *split(table), dims)


def dot_split(x, t_high, t_low, dims):
    count = x.shape[0]
    x_high, x_low = split(x)
    main = lax.dot_general(jnp.concatenate([x_high, x_low]), t_high, dims, preferred_element_type=F32)
    rest = lax.dot_general(x_high, t_low, dims, preferred_element_type=F32)
    return main[:count] + (main[count:] + rest)


def merged(basis):
    return basis.reshape(-1, basis.shape[-1])


def chunks_of(rank):
    widths = [LANES] * (rank // LANES)
    return widths + [w for w in (1 << b for b in reversed(range(LANES.bit_length() - 1))) if rank % LANES & w]


def packed_rows(cols, rank):
    return cols * rank // LANES


def pack(block):
    cols, rank = block.shape
    out, at = [], 0
    for w in chunks_of(rank):
        rows = cols * w // LANES
        piece = block[:, at : at + w]
        out.append(jnp.concatenate([piece[r : r + rows] for r in range(0, cols, rows)], axis=1))
        at += w
    return jnp.concatenate(out)


def unpack(dense, cols):
    out, at = [], 0
    for w in chunks_of(dense.shape[0] * LANES // cols):
        rows = cols * w // LANES
        piece = dense[at : at + rows]
        out.append(jnp.concatenate([piece[:, l : l + w] for l in range(0, LANES, w)]))
        at += rows
    return jnp.concatenate(out, axis=1)


def side_by_side(coefs, cols):
    return jnp.concatenate([unpack(coefs[l], cols) for l in range(coefs.shape[0])], axis=1)


def store_levels(ref, wide_block):
    rank = wide_block.shape[1] // ref.shape[0]
    for l in range(ref.shape[0]):
        ref[l] = pack(wide_block[:, l * rank : (l + 1) * rank])


def leaf_slices(blocks):
    leaf, rows = blocks.shape
    return [slice(s, s + leaf) for s in range(0, rows, leaf)]


def near_kernel(field, incident, leaf_blocks, col_basis, row_basis, near):
    pieces = leaf_slices(leaf_blocks)
    coefs = [dot(field[:, s], row_basis[0, :, s], ROWS_OF_BOTH) for s in pieces]
    for k, s in enumerate(pieces):
        image = dot(field[:, s], leaf_blocks[:, s], PLAIN)
        near[:, s] = incident[:, s] - image - dot(coefs[k ^ 1], col_basis[0, :, s], PLAIN)


def near_and_copy_kernel(field, incident, leaf_blocks, col_basis, row_basis, near, copy):
    copy[...] = field[...]
    near_kernel(field, incident, leaf_blocks, col_basis, row_basis, near)


def first_top_kernel(field_hbm, row_hbm, top, field, row, sems):
    levels = row_hbm.shape[0]
    copies = [pltpu.make_async_copy(field_hbm, field, sems.at[levels])]
    copies += [pltpu.make_async_copy(row_hbm.at[l], row.at[l], sems.at[l]) for l in reversed(range(levels))]
    for c in copies:
        c.start()
    for c in copies[: TOP + 1]:
        c.wait()
    store_levels(top, dot(field[...], merged(row[levels - TOP :]), ROWS_OF_BOTH))
    for c in copies[TOP + 1 :]:
        c.wait()


def low_kernel(field, row_basis, low):
    store_levels(low, dot(field[...], merged(row_basis[1 : row_basis.shape[0] - TOP]), ROWS_OF_BOTH))


def apply_kernel(start, near, coefs, col_basis, out):
    table = merged(col_basis[start : start + coefs.shape[0]])
    out[...] = near[...] - dot(side_by_side(coefs, near.shape[0]), table, PLAIN)


def near_and_tables_kernel(
    start,
    field,
    incident,
    leaf_blocks,
    col_basis,
    row_basis,
    inverse_hbm,
    near,
    leaf_inverse,
    mixed_high,
    mixed_low,
    top_high,
    top_low,
    sem,
):
    copy = pltpu.make_async_copy(inverse_hbm, leaf_inverse, sem)
    copy.start()
    near_kernel(field, incident, leaf_blocks, col_basis, row_basis, near)
    copy.wait()
    for s in leaf_slices(leaf_inverse):
        mixed = dot(merged(col_basis[start:, :, s]), leaf_inverse[:, s], PLAIN)
        mixed_high[:, s], mixed_low[:, s] = split(mixed)
    top_high[...], top_low[...] = split(merged(row_basis[row_basis.shape[0] - TOP :]))


def apply_and_base_kernel(start, near, coefs, col_basis, field, leaf_inverse, base):
    table = merged(col_basis[start : start + coefs.shape[0]])
    first = near[...] - dot(side_by_side(coefs, near.shape[0]), table, PLAIN)
    for s in leaf_slices(leaf_inverse):
        base[:, s] = field[:, s] + dot(first[:, s], leaf_inverse[:, s], PLAIN)


def refine_kernel(base, coefs, mixed_high, mixed_low, top_high, top_low, refined, top):
    refined[...] = base[...] - dot_split(
        side_by_side(coefs, base.shape[0]), mixed_high[...], mixed_low[...], PLAIN
    )
    store_levels(top, dot_split(refined[...], top_high[...], top_low[...], ROWS_OF_BOTH))


def last_kernel(start, near, coefs, col_basis, out_hbm, out, sems):
    coefs = side_by_side(coefs, near.shape[0])
    rows = near.shape[1]
    step = rows // sems.shape[0]
    copies = []
    for k in range(sems.shape[0]):
        s = slice(k * step, k * step + step)
        out[:, s] = near[:, s] - dot(coefs, merged(col_basis[start:, :, s]), PLAIN)
        copies.append(pltpu.make_async_copy(out.at[:, s], out_hbm.at[:, s], sems.at[k]))
        copies[-1].start()
    for c in copies:
        c.wait()


def run(kernel, outs, *args, cycles=None):
    whole = pl.BlockSpec(memory_space=VMEM)
    return pl.pallas_call(
        kernel,
        out_shape=[VMEM(shape, kind) if inside else jax.ShapeDtypeStruct(shape, kind) for shape, inside, kind in outs],
        in_specs=[whole] * len(args),
        out_specs=[whole] * len(outs),
        compiler_params=pltpu.CompilerParams(vmem_limit_bytes=24 << 20),
    )(*[pltpu.with_memory_space_constraint(a, VMEM) for a in args])


def per_device(solution, incident, leaf_blocks, leaf_inverse, col_basis, row_basis):
    solution, first = lax.optimization_barrier((solution, in_first_lane()))
    levels, rank, rows = row_basis.shape
    cols = solution.shape[0]
    dense = (packed_rows(cols, rank), LANES)
    in_field = ((cols, rows), True, F32)
    low_out = ((levels - 1 - TOP, *dense), True, F32)
    top_out = ((TOP, *dense), True, F32)
    in_vmem = pl.BlockSpec(memory_space=VMEM)
    in_hbm = pl.BlockSpec(memory_space=pltpu.HBM)
    params = pltpu.CompilerParams(vmem_limit_bytes=24 << 20)
    top, field, row_basis = pl.pallas_call(
        first_top_kernel,
        out_shape=[VMEM(top_out[0], F32), VMEM(solution.shape, F32), VMEM(row_basis.shape, F32)],
        in_specs=[in_hbm] * 2,
        out_specs=[in_vmem] * 3,
        scratch_shapes=[pltpu.SemaphoreType.DMA((levels + 1,))],
        compiler_params=params,
    )(*[pltpu.with_memory_space_constraint(a, pltpu.HBM) for a in (solution, row_basis)])
    (low,) = run(low_kernel, [low_out], field, row_basis)

    late = levels - TOP
    mixed_out = (((levels - late) * rank, rows), True, jnp.bfloat16)
    split_out = ((TOP * rank, rows), True, jnp.bfloat16)

    def near_and_tables():
        outs = [in_field, (leaf_inverse.shape, True, F32), mixed_out, mixed_out, split_out, split_out]
        in_place = [pltpu.with_memory_space_constraint(a, VMEM) for a in (field, incident, leaf_blocks, col_basis, row_basis)]
        return pl.pallas_call(
            functools.partial(near_and_tables_kernel, late),
            out_shape=[VMEM(shape, kind) for shape, _, kind in outs],
            in_specs=[in_vmem] * 5 + [in_hbm],
            out_specs=[in_vmem] * len(outs),
            scratch_shapes=[pltpu.SemaphoreType.DMA],
            compiler_params=params,
        )(*in_place, pltpu.with_memory_space_constraint(leaf_inverse, pltpu.HBM))

    def apply_and_base(start, near, coefs, inverse, *_):
        kernel = functools.partial(apply_and_base_kernel, start)
        return run(kernel, [in_field], near, coefs, col_basis, field, inverse)[0]

    def near_and_copy():
        outs = [in_field, ((cols, rows), False, F32)]
        return run(near_and_copy_kernel, outs, refined, incident, leaf_blocks, col_basis, row_basis)

    def apply(start, near, coefs, *_):
        return run(functools.partial(apply_kernel, start), [in_field], near, coefs, col_basis)[0]

    base, start, coefs, tables = exchange(first, low, top, near_and_tables, apply_and_base)
    refined, top = run(refine_kernel, [in_field, top_out], base, coefs, *tables[1:])
    (low,) = run(low_kernel, [low_out], refined, row_basis)
    near, start, coefs, others = exchange(first, low, top, near_and_copy, apply)
    residual = pl.pallas_call(
        functools.partial(last_kernel, start),
        out_shape=jax.ShapeDtypeStruct((cols, rows), F32),
        in_specs=[in_vmem] * 3,
        out_specs=in_hbm,
        scratch_shapes=[VMEM((cols, rows), F32), pltpu.SemaphoreType.DMA((4,))],
        compiler_params=params,
    )(*[pltpu.with_memory_space_constraint(a, VMEM) for a in (near, coefs, col_basis)])
    return (others[0], residual)


def solution(mesh):
    in_specs = (
        P(None, ("wide", "grp")),
        P(None, ("wide", "grp")),
        P(None, ("wide", "grp")),
        P(None, ("wide", "grp")),
        P(None, None, ("wide", "grp")),
        P(None, None, ("wide", "grp")),
    )
    out_specs = (P(None, ("wide", "grp")), P(None, ("wide", "grp")))
    return jax.shard_map(
        per_device, mesh=mesh, in_specs=in_specs, out_specs=out_specs, check_vma=False
    )
```
